32 devices in a mesh: strip: 32 (over z, y, x, core).
Axes of the slice: x: 2, y: 2, z: 4, core: 2. Of those that a mesh axis runs over, the one named last changes fastest.
Arguments:
- velocity: float32 [2, 128, 128, 768], P(None, None, 'strip'), may hold values from -100 to 100
Outputs:
- spatial_modes: float32 [128, 128, 768], P(None, 'strip')
- triangle: float32 [128, 128], replicated
The draws below stay inside these ranges and needn't reach their ends.
All inputs are finite; a program needn't handle non-finite values.
Results may differ from the reference program's by a relative error of at most 0.000094.
Values sent between devices are 32-bit elements; how exact they have to be, the bound alone decides.
A program may use at most 128 MiB of HBM per device.

```python
import math
import jax
import jax.numpy as jnp
from jax import lax

K = 128
NY = 768
NX = 128


def draw_velocity(key, part):
    keys = jax.random.split(key, 4)
    snap_scale = jnp.exp(jax.random.uniform(keys[0], (1, K, 1, 1), jnp.float32, math.log(0.5), math.log(5.0)))
    row_scale = jnp.exp(jax.random.uniform(keys[1], (1, 1, NX, 1), jnp.float32, math.log(0.5), math.log(1.6)))
    col_scale = jnp.exp(jax.random.uniform(keys[2], (1, 1, 1, NY), jnp.float32, math.log(0.5), math.log(1.6)))
    noise = jnp.clip(jax.random.normal(keys[3], (2, K, NX, NY), jnp.float32), -6.0, 6.0)
    return (noise * snap_scale * row_scale * col_scale).astype(jnp.float32)


def setup_inputs(seed: int = 0) -> dict:
    arg_keys = jax.random.split(jax.random.key(seed), 2)
    return {
        "velocity": draw_velocity(jax.random.fold_in(arg_keys[1], 71), 0),
    }


def along_first(field):
    return (8.0 * (jnp.roll(field, -1, 0) - jnp.roll(field, 1, 0)) - (jnp.roll(field, -2, 0) - jnp.roll(field, 2, 0))) / 12.0

def along_second(field):
    return (8.0 * (jnp.roll(field, -1, 1) - jnp.roll(field, 1, 1)) - (jnp.roll(field, -2, 1) - jnp.roll(field, 2, 1))) / 12.0

def reference(velocity):
    zero_index = jnp.zeros((), jnp.int32)
    one_index = jnp.ones((), jnp.int32)

    def one_snapshot(snap_index):
        comp_u = lax.dynamic_slice(velocity, (zero_index, snap_index, zero_index, zero_index), (1, 1, NX, NY))[0, 0]
        comp_v = lax.dynamic_slice(velocity, (one_index, snap_index, zero_index, zero_index), (1, 1, NX, NY))[0, 0]
        return along_first(comp_v) - along_second(comp_u)
    vorticity = lax.map(one_snapshot, jnp.arange(K, dtype=jnp.int32))
    flattened = vorticity.reshape(K, NX * NY)
    gram = jnp.dot(flattened.astype(jnp.float32), flattened.T.astype(jnp.float32), precision=lax.Precision.HIGHEST, preferred_element_type=jnp.float32) / (NX * NY)
    lower = jnp.linalg.cholesky(gram)
    spatial_modes = lax.linalg.triangular_solve(lower, flattened, left_side=True, lower=True)
    return (spatial_modes.reshape(K, NX, NY), lower.T)
```

```python
import functools

import jax
import jax.numpy as jnp
from jax import lax
from jax.experimental import pallas as pl
from jax.experimental.pallas import tpu as pltpu
from jax.sharding import PartitionSpec as P

LANES = 128
HIGHEST = lax.Precision.HIGHEST
MESH = pl.DeviceIdType.MESH


def gram_kernel(
    n, snaps, rows, chunks, group, scale,
    vel_ref, w_ref, gram_ref,
    vel, field, before, after, part, piece, gathered,
    load_sem, up_send, up_recv, down_send, down_recv,
    scatter_send, scatter_recv, cross_send, cross_recv, gather_send, gather_recv,
):
    me = lax.axis_index("strip")
    right, left = lax.rem(me + 1, n), lax.rem(me + n - 1, n)
    in_group = lax.rem(me, group)
    base = me - in_group
    group_id = me // group
    groups = n // group
    height = snaps // group
    stride = rows * chunks

    loads = [
        pltpu.make_async_copy(vel_ref.at[c], vel.at[c], load_sem.at[c]) for c in (1, 0)
    ]
    for load in loads:
        load.start()

    def group_peer(offset):
        return base + lax.rem(in_group + offset, group)

    def cross_peer(offset):
        return lax.rem(me + offset * group, n)

    barrier = pltpu.get_barrier_semaphore()
    greeted = [right, left]
    greeted += [group_peer(o) for o in range(1, group)]
    greeted += [cross_peer(o) for o in range(1, groups)]
    for peer in greeted:
        pl.semaphore_signal(barrier, inc=1, device_id=(peer,), device_id_type=MESH)
    loads[0].wait()
    for t in range(chunks):
        for r in range(rows):
            field[t, r] = vel[1, pl.ds(t * rows + r, snaps, stride=stride), :]
        if t == 0:
            pl.semaphore_wait(barrier, len(greeted))
        for src, dst, peer, send, recv in (
            (field.at[t, pl.ds(rows - 2, 2)], before.at[t], right, up_send, up_recv),
            (field.at[t, pl.ds(0, 2)], after.at[t], left, down_send, down_recv),
        ):
            pltpu.make_async_remote_copy(
                src_ref=src, dst_ref=dst, send_sem=send.at[t], recv_sem=recv.at[t],
                device_id=(peer,), device_id_type=MESH,
            ).start()

    loads[1].wait()
    step = 16
    cols = chunks * LANES

    @pl.loop(0, snaps // step)
    def _(block):
        first = block * step
        for r in range(rows):
            row = jnp.concatenate(
                [
                    vel[0, pl.ds(first * stride + t * rows + r, step, stride=stride), :]
                    for t in range(chunks)
                ],
                axis=1,
            )
            wide = row - pltpu.roll(row, 2, 1)
            nine = 8.0 * wide - pltpu.roll(wide, cols - 1, 1)
            along = pltpu.roll(nine, cols - 1, 1) - wide
            for t in range(chunks):
                here = pl.ds(first, step)
                out = -along[:, t * LANES : (t + 1) * LANES]
                for shift, weight in ((1, 8.0), (-1, -8.0), (2, -1.0), (-2, 1.0)):
                    if 0 <= r + shift < rows:
                        out = out + weight * field[t, r + shift, here]
                w_ref[t, r, here] = out

    for t in range(chunks):
        up = pltpu.make_async_remote_copy(
            src_ref=field.at[t, pl.ds(rows - 2, 2)], dst_ref=before.at[t],
            send_sem=up_send.at[t], recv_sem=up_recv.at[t],
            device_id=(right,), device_id_type=MESH,
        )
        down = pltpu.make_async_remote_copy(
            src_ref=field.at[t, pl.ds(0, 2)], dst_ref=after.at[t],
            send_sem=down_send.at[t], recv_sem=down_recv.at[t],
            device_id=(left,), device_id_type=MESH,
        )
        up.wait()
        down.wait()
        for r in range(rows):
            out = w_ref[t, r]
            for shift, weight in ((1, 8.0), (-1, -8.0), (2, -1.0), (-2, 1.0)):
                if r + shift < 0:
                    out = out + weight * before[t, r + shift + 2]
                elif r + shift >= rows:
                    out = out + weight * after[t, r + shift - rows]
            w_ref[t, r] = out
            term = lax.dot_general(
                out, out, (((1,), (1,)), ((), ())),
                precision=HIGHEST, preferred_element_type=jnp.float32,
            )
            if t == 0 and r == 0:
                part[...] = term
            else:
                part[...] += term

    copies = []
    for o in range(1, group):
        other = lax.rem(in_group + o, group)
        copy = pltpu.make_async_remote_copy(
            src_ref=part.at[pl.ds(pl.multiple_of(other * height, 8), height)],
            dst_ref=piece.at[o - 1],
            send_sem=scatter_send.at[o - 1], recv_sem=scatter_recv.at[o - 1],
            device_id=(group_peer(o),), device_id_type=MESH,
        )
        copy.start()
        copies.append(copy)
    mine = pl.ds(pl.multiple_of(in_group * height, 8), height)
    total = part[mine, :]
    for o in range(1, group):
        copies[o - 1].wait()
        total = total + piece[o - 1]
    if groups > 1:
        gathered[group_id] = total
        copies = []
        for o in range(1, groups):
            copy = pltpu.make_async_remote_copy(
                src_ref=gathered.at[group_id], dst_ref=gathered.at[group_id],
                send_sem=cross_send.at[o - 1], recv_sem=cross_recv.at[o - 1],
                device_id=(cross_peer(o),), device_id_type=MESH,
            )
            copy.start()
            copies.append(copy)
        for copy in copies:
            copy.wait()
        total = gathered[0]
        for g in range(1, groups):
            total = total + gathered[g]
    gram_ref[mine, :] = total * scale
    copies = []
    for o in range(1, group):
        copy = pltpu.make_async_remote_copy(
            src_ref=gram_ref.at[mine], dst_ref=gram_ref.at[mine],
            send_sem=gather_send.at[o - 1], recv_sem=gather_recv.at[o - 1],
            device_id=(group_peer(o),), device_id_type=MESH,
        )
        copy.start()
        copies.append(copy)
    for copy in copies:
        copy.wait()


def tiles_first(array):
    *lead, rows, cols = array.shape
    array = array.reshape(*lead, rows, cols // LANES, LANES)
    array = jnp.swapaxes(array, -3, -2)
    return array


def vorticity_gram(velocity, n):
    _, snaps, rows, cols = velocity.shape
    chunks = cols // LANES
    group = 8
    groups = n // group
    height = snaps // group
    scale = 1.0 / (144.0 * n * rows * cols)
    flat = tiles_first(velocity).reshape(2, snaps * chunks * rows, LANES)
    dma = pltpu.SemaphoreType.DMA
    f32 = jnp.float32
    vmem = pl.BlockSpec(memory_space=pltpu.VMEM)
    return pl.pallas_call(
        functools.partial(gram_kernel, n, snaps, rows, chunks, group, scale),
        out_shape=(
            jax.ShapeDtypeStruct((chunks, rows, snaps, LANES), f32),
            jax.ShapeDtypeStruct((snaps, snaps), f32),
        ),
        in_specs=[pl.BlockSpec(memory_space=pl.ANY)],
        out_specs=(vmem, vmem),
        scratch_shapes=[
            pltpu.VMEM((2, snaps * chunks * rows, LANES), f32),
            pltpu.VMEM((chunks, rows, snaps, LANES), f32),
            pltpu.VMEM((chunks, 2, snaps, LANES), f32),
            pltpu.VMEM((chunks, 2, snaps, LANES), f32),
            pltpu.VMEM((snaps, snaps), f32),
            pltpu.VMEM((group - 1, height, snaps), f32),
            pltpu.VMEM((groups, height, snaps), f32),
            dma((2,)),
            dma((chunks,)), dma((chunks,)), dma((chunks,)), dma((chunks,)),
            dma((group - 1,)), dma((group - 1,)),
            dma((max(groups - 1, 1),)), dma((max(groups - 1, 1),)),
            dma((group - 1,)), dma((group - 1,)),
        ],
        compiler_params=pltpu.CompilerParams(
            collective_id=0, has_side_effects=True, vmem_limit_bytes=32 * 1024 * 1024
        ),
        name="vorticity_gram",
    )(flat)


def local(n, velocity):
    _, snaps, rows, cols = velocity.shape
    chunks = cols // LANES
    w, gram = vorticity_gram(velocity, n)
    lower = jnp.linalg.cholesky(gram)
    identity = jnp.eye(snaps, dtype=jnp.float32)
    inverse = lax.linalg.triangular_solve(lower, identity, left_side=True, lower=True)
    modes = lax.dot_general(
        inverse * (1.0 / 12.0), w, (((1,), (2,)), ((), ())),
        precision=HIGHEST, preferred_element_type=jnp.float32,
    )
    modes = jnp.transpose(modes, (0, 2, 1, 3)).reshape(snaps, rows, cols)
    return modes, lower.T


def solution(mesh):
    return jax.shard_map(
        functools.partial(local, mesh.shape["strip"]),
        mesh=mesh,
        in_specs=(P(None, None, "strip", None),),
        out_specs=(P(None, "strip", None), P()),
        check_vma=False,
    )
```

```python
import functools

import jax
import jax.numpy as jnp
from jax import lax
from jax.experimental import pallas as pl
from jax.experimental.pallas import tpu as pltpu
from jax.experimental.layout import Layout, with_layout_constraint
from jax.sharding import PartitionSpec as P

LANES = 128
HIGHEST = lax.Precision.HIGHEST
MESH = pl.DeviceIdType.MESH


def gram_kernel(
    n, snaps, rows, chunks, group, scale,
    vel_ref, w_ref, gram_ref,
    vel, field, before, after, part, piece, gathered,
    load_sem, up_send, up_recv, down_send, down_recv,
    scatter_send, scatter_recv, cross_send, cross_recv, gather_send, gather_recv,
):
    me = lax.axis_index("strip")
    right, left = lax.rem(me + 1, n), lax.rem(me + n - 1, n)
    in_group = lax.rem(me, group)
    base = me - in_group
    group_id = me // group
    groups = n // group
    height = snaps // group
    stride = rows * chunks

    loads = [
        pltpu.make_async_copy(vel_ref.at[c], vel.at[c], load_sem.at[c]) for c in (1, 0)
    ]
    for load in loads:
        load.start()

    def group_peer(offset):
        return base + lax.rem(in_group + offset, group)

    def cross_peer(offset):
        return lax.rem(me + offset * group, n)

    barrier = pltpu.get_barrier_semaphore()
    greeted = [right, left]
    greeted += [group_peer(o) for o in range(1, group)]
    greeted += [cross_peer(o) for o in range(1, groups)]
    for peer in greeted:
        pl.semaphore_signal(barrier, inc=1, device_id=(peer,), device_id_type=MESH)
    loads[0].wait()
    for t in range(chunks):
        for r in range(rows):
            field[t, r] = vel[1, pl.ds(t * rows + r, snaps, stride=stride), :]
        if t == 0:
            pl.semaphore_wait(barrier, len(greeted))
        for src, dst, peer, send, recv in (
            (field.at[t, pl.ds(rows - 2, 2)], before.at[t], right, up_send, up_recv),
            (field.at[t, pl.ds(0, 2)], after.at[t], left, down_send, down_recv),
        ):
            pltpu.make_async_remote_copy(
                src_ref=src, dst_ref=dst, send_sem=send.at[t], recv_sem=recv.at[t],
                device_id=(peer,), device_id_type=MESH,
            ).start()

    loads[1].wait()
    step = 16
    cols = chunks * LANES

    @pl.loop(0, snaps // step)
    def _(block):
        first = block * step
        for r in range(rows):
            row = jnp.concatenate(
                [
                    vel[0, pl.ds(first * stride + t * rows + r, step, stride=stride), :]
                    for t in range(chunks)
                ],
                axis=1,
            )
            wide = row - pltpu.roll(row, 2, 1)
            nine = 8.0 * wide - pltpu.roll(wide, cols - 1, 1)
            along = pltpu.roll(nine, cols - 1, 1) - wide
            for t in range(chunks):
                here = pl.ds(first, step)
                out = -along[:, t * LANES : (t + 1) * LANES]
                for shift, weight in ((1, 8.0), (-1, -8.0), (2, -1.0), (-2, 1.0)):
                    if 0 <= r + shift < rows:
                        out = out + weight * field[t, r + shift, here]
                w_ref[t, r, here] = out

    for t in range(chunks):
        up = pltpu.make_async_remote_copy(
            src_ref=field.at[t, pl.ds(rows - 2, 2)], dst_ref=before.at[t],
            send_sem=up_send.at[t], recv_sem=up_recv.at[t],
            device_id=(right,), device_id_type=MESH,
        )
        down = pltpu.make_async_remote_copy(
            src_ref=field.at[t, pl.ds(0, 2)], dst_ref=after.at[t],
            send_sem=down_send.at[t], recv_sem=down_recv.at[t],
            device_id=(left,), device_id_type=MESH,
        )
        up.wait()
        down.wait()
        for r in range(rows):
            out = w_ref[t, r]
            for shift, weight in ((1, 8.0), (-1, -8.0), (2, -1.0), (-2, 1.0)):
                if r + shift < 0:
                    out = out + weight * before[t, r + shift + 2]
                elif r + shift >= rows:
                    out = out + weight * after[t, r + shift - rows]
            w_ref[t, r] = out
            term = lax.dot_general(
                out, out, (((1,), (1,)), ((), ())),
                precision=HIGHEST, preferred_element_type=jnp.float32,
            )
            if t == 0 and r == 0:
                part[...] = term
            else:
                part[...] += term

    copies = []
    for o in range(1, group):
        other = lax.rem(in_group + o, group)
        copy = pltpu.make_async_remote_copy(
            src_ref=part.at[pl.ds(pl.multiple_of(other * height, 8), height)],
            dst_ref=piece.at[o - 1],
            send_sem=scatter_send.at[o - 1], recv_sem=scatter_recv.at[o - 1],
            device_id=(group_peer(o),), device_id_type=MESH,
        )
        copy.start()
        copies.append(copy)
    mine = pl.ds(pl.multiple_of(in_group * height, 8), height)
    total = part[mine, :]
    for o in range(1, group):
        copies[o - 1].wait()
        total = total + piece[o - 1]
    if groups > 1:
        gathered[group_id] = total
        copies = []
        for o in range(1, groups):
            copy = pltpu.make_async_remote_copy(
                src_ref=gathered.at[group_id], dst_ref=gathered.at[group_id],
                send_sem=cross_send.at[o - 1], recv_sem=cross_recv.at[o - 1],
                device_id=(cross_peer(o),), device_id_type=MESH,
            )
            copy.start()
            copies.append(copy)
        for copy in copies:
            copy.wait()
        total = gathered[0]
        for g in range(1, groups):
            total = total + gathered[g]
    gram_ref[mine, :] = total * scale
    copies = []
    for o in range(1, group):
        copy = pltpu.make_async_remote_copy(
            src_ref=gram_ref.at[mine], dst_ref=gram_ref.at[mine],
            send_sem=gather_send.at[o - 1], recv_sem=gather_recv.at[o - 1],
            device_id=(group_peer(o),), device_id_type=MESH,
        )
        copy.start()
        copies.append(copy)
    for copy in copies:
        copy.wait()


def tiles_first(array):
    *lead, rows, cols = array.shape
    array = array.reshape(*lead, rows, cols // LANES, LANES)
    k = len(lead)
    order = tuple(range(k)) + (k + 1, k, k + 2)
    array = with_layout_constraint(array, Layout(major_to_minor=order))
    return jnp.swapaxes(array, -3, -2)


def vorticity_gram(velocity, n):
    _, snaps, rows, cols = velocity.shape
    chunks = cols // LANES
    group = 8
    groups = n // group
    height = snaps // group
    scale = 1.0 / (144.0 * n * rows * cols)
    flat = tiles_first(velocity).reshape(2, snaps * chunks * rows, LANES)
    dma = pltpu.SemaphoreType.DMA
    f32 = jnp.float32
    vmem = pl.BlockSpec(memory_space=pltpu.VMEM)
    return pl.pallas_call(
        functools.partial(gram_kernel, n, snaps, rows, chunks, group, scale),
        out_shape=(
            jax.ShapeDtypeStruct((chunks, rows, snaps, LANES), f32),
            jax.ShapeDtypeStruct((snaps, snaps), f32),
        ),
        in_specs=[pl.BlockSpec(memory_space=pl.ANY)],
        out_specs=(vmem, vmem),
        scratch_shapes=[
            pltpu.VMEM((2, snaps * chunks * rows, LANES), f32),
            pltpu.VMEM((chunks, rows, snaps, LANES), f32),
            pltpu.VMEM((chunks, 2, snaps, LANES), f32),
            pltpu.VMEM((chunks, 2, snaps, LANES), f32),
            pltpu.VMEM((snaps, snaps), f32),
            pltpu.VMEM((group - 1, height, snaps), f32),
            pltpu.VMEM((groups, height, snaps), f32),
            dma((2,)),
            dma((chunks,)), dma((chunks,)), dma((chunks,)), dma((chunks,)),
            dma((group - 1,)), dma((group - 1,)),
            dma((max(groups - 1, 1),)), dma((max(groups - 1, 1),)),
            dma((group - 1,)), dma((group - 1,)),
        ],
        compiler_params=pltpu.CompilerParams(
            collective_id=0, has_side_effects=True, vmem_limit_bytes=58 * 1024 * 1024
        ),
        name="vorticity_gram",
    )(flat)


def modes_kernel(
    snaps, rows, chunks, parts, gram_ref, w_ref, out_ref, triangle_ref, inverse, out, out_sem
):
    blocks = snaps // 8
    sub = lax.broadcasted_iota(jnp.int32, (8, snaps), 0)
    lane = lax.broadcasted_iota(jnp.int32, (8, snaps), 1)
    left = [gram_ref[pl.ds(8 * b, 8), :] for b in range(blocks)]
    side = [jnp.where(lane == sub + 8 * b, 1.0, 0.0) for b in range(blocks)]

    for b in range(blocks):
        spread = [
            [jnp.broadcast_to(left[i][:, 8 * b + k : 8 * b + k + 1], (8, snaps)) for k in range(8)]
            for i in range(b, blocks)
        ]
        pivots = spread[0][0]
        for k in range(8):
            pivot = spread[0][k][k : k + 1, :]
            inv = 1.0 / pivot
            pivots = jnp.where(sub == k, spread[0][k], pivots)
            row_left = left[b][k : k + 1, :]
            row_side = side[b][k : k + 1, :]
            row_spread = [spread[0][q][k : k + 1, :] for q in range(k + 1, 8)]
            for i in range(b, blocks):
                mult = spread[i - b][k] * inv
                if i == b:
                    mult = jnp.where(sub > k, mult, 0.0)
                if i > b or k < 7:
                    left[i] = left[i] - mult * row_left
                    side[i] = side[i] - mult * row_side
                    for q in range(k + 1, 8):
                        spread[i - b][q] = spread[i - b][q] - mult * row_spread[q - k - 1]
        root = lax.rsqrt(pivots)
        here = pl.ds(8 * b, 8)
        triangle_ref[here, :] = jnp.where(lane >= sub + 8 * b, left[b] * root, 0.0)
        inverse[here, :] = side[b] * (root * (1.0 / 12.0))

    size = snaps // parts
    span = size * rows * chunks
    copies = []
    for p in range(parts):
        mine = inverse[pl.ds(p * size, size), :]
        for t in range(chunks):
            for r in range(rows):
                out[pl.ds(p * span + t * rows + r, size, stride=rows * chunks), :] = jnp.dot(
                    mine, w_ref[t, r], precision=HIGHEST, preferred_element_type=jnp.float32
                )
        copy = pltpu.make_async_copy(
            out.at[pl.ds(p * span, span)], out_ref.at[pl.ds(p * span, span)], out_sem.at[p]
        )
        copy.start()
        copies.append(copy)
    for copy in copies:
        copy.wait()


def modes_triangle(gram, w):
    chunks, rows, snaps, _ = w.shape
    parts = 2
    f32 = jnp.float32
    vmem = pl.BlockSpec(memory_space=pltpu.VMEM)
    return pl.pallas_call(
        functools.partial(modes_kernel, snaps, rows, chunks, parts),
        out_shape=(
            jax.ShapeDtypeStruct((snaps * chunks * rows, LANES), f32),
            jax.ShapeDtypeStruct((snaps, snaps), f32),
        ),
        in_specs=[vmem, vmem],
        out_specs=(pl.BlockSpec(memory_space=pl.ANY), vmem),
        scratch_shapes=[
            pltpu.VMEM((snaps, snaps), f32),
            pltpu.VMEM((snaps * chunks * rows, LANES), f32),
            pltpu.SemaphoreType.DMA((parts,)),
        ],
        compiler_params=pltpu.CompilerParams(vmem_limit_bytes=58 * 1024 * 1024),
        name="modes_triangle",
    )(gram, w)


def rows_first(array, snaps, rows, chunks):
    array = array.reshape(snaps, chunks, rows, LANES)
    array = jnp.swapaxes(array, 1, 2)
    array = with_layout_constraint(array, Layout(major_to_minor=(0, 2, 1, 3)))
    return array.reshape(snaps, rows, chunks * LANES)


def local(n, velocity):
    _, snaps, rows, cols = velocity.shape
    w, gram = vorticity_gram(velocity, n)
    modes, triangle = modes_triangle(gram, w)
    return rows_first(modes, snaps, rows, cols // LANES), triangle


def solution(mesh):
    return jax.shard_map(
        functools.partial(local, mesh.shape["strip"]),
        mesh=mesh,
        in_specs=(P(None, None, "strip", None),),
        out_specs=(P(None, "strip", None), P()),
        check_vma=False,
    )
```

```python
import functools

import jax
import jax.numpy as jnp
from jax import lax
from jax.experimental import pallas as pl
from jax.experimental.pallas import tpu as pltpu
from jax.experimental.layout import Layout, with_layout_constraint
from jax.sharding import PartitionSpec as P

LANES = 128
GROUP = 8
HIGHEST = lax.Precision.HIGHEST
MESH = pl.DeviceIdType.MESH


def gram_kernel(
    n, snaps, rows, chunks, group, scale,
    vel_ref, w_out, gram_ref,
    w_ref, vel, field, before, after, part, piece, gathered,
    load_sem, w_sem, up_send, up_recv, down_send, down_recv,
    scatter_send, scatter_recv, cross_send, cross_recv, gather_send, gather_recv,
):
    me = lax.axis_index("strip")
    right, left = lax.rem(me + 1, n), lax.rem(me + n - 1, n)
    in_group = lax.rem(me, group)
    base = me - in_group
    group_id = me // group
    groups = n // group
    stride = rows * chunks

    loads = [
        pltpu.make_async_copy(vel_ref.at[c], vel.at[c], load_sem.at[c]) for c in (1, 0)
    ]
    loads[0].start()

    def group_peer(offset):
        return base + lax.rem(in_group + offset, group)

    def cross_peer(offset):
        return lax.rem(me + offset * group, n)

    barrier = pltpu.get_barrier_semaphore()
    greeted = [right, left]
    greeted += [group_peer(o) for o in range(1, group)]
    greeted += [cross_peer(o) for o in range(1, groups)]
    for peer in greeted:
        pl.semaphore_signal(barrier, inc=1, device_id=(peer,), device_id_type=MESH)
    loads[0].wait()
    for t in range(chunks):
        for r in range(rows):
            field[t, r] = vel[1, pl.ds(t * rows + r, snaps, stride=stride), :]
        if t == 0:
            pl.semaphore_wait(barrier, len(greeted))
        for src, dst, peer, send, recv in (
            (field.at[t, pl.ds(rows - 2, 2)], before.at[t], right, up_send, up_recv),
            (field.at[t, pl.ds(0, 2)], after.at[t], left, down_send, down_recv),
        ):
            pltpu.make_async_remote_copy(
                src_ref=src, dst_ref=dst, send_sem=send.at[t], recv_sem=recv.at[t],
                device_id=(peer,), device_id_type=MESH,
            ).start()
        if t == 0:
            loads[1].start()

    loads[1].wait()
    step = 16
    cols = chunks * LANES

    @pl.loop(0, snaps // step)
    def _(block):
        first = block * step
        for r in range(rows):
            row = jnp.concatenate(
                [
                    vel[0, pl.ds(first * stride + t * rows + r, step, stride=stride), :]
                    for t in range(chunks)
                ],
                axis=1,
            )
            wide = row - pltpu.roll(row, 2, 1)
            nine = 8.0 * wide - pltpu.roll(wide, cols - 1, 1)
            along = pltpu.roll(nine, cols - 1, 1) - wide
            for t in range(chunks):
                here = pl.ds(first, step)
                out = -along[:, t * LANES : (t + 1) * LANES]
                for shift, weight in ((1, 8.0), (-1, -8.0), (2, -1.0), (-2, 1.0)):
                    if 0 <= r + shift < rows:
                        out = out + weight * field[t, r + shift, here]
                w_ref[t, r, here] = out

    sent = []
    for t in range(chunks):
        up = pltpu.make_async_remote_copy(
            src_ref=field.at[t, pl.ds(rows - 2, 2)], dst_ref=before.at[t],
            send_sem=up_send.at[t], recv_sem=up_recv.at[t],
            device_id=(right,), device_id_type=MESH,
        )
        down = pltpu.make_async_remote_copy(
            src_ref=field.at[t, pl.ds(0, 2)], dst_ref=after.at[t],
            send_sem=down_send.at[t], recv_sem=down_recv.at[t],
            device_id=(left,), device_id_type=MESH,
        )
        up.wait_recv()
        down.wait_recv()
        sent += [up, down]
        for r in range(rows):
            out = w_ref[t, r]
            for shift, weight in ((1, 8.0), (-1, -8.0), (2, -1.0), (-2, 1.0)):
                if r + shift < 0:
                    out = out + weight * before[t, r + shift + 2]
                elif r + shift >= rows:
                    out = out + weight * after[t, r + shift - rows]
            w_ref[t, r] = out
            term = lax.dot_general(
                out, out, (((1,), (1,)), ((), ())),
                precision=HIGHEST, preferred_element_type=jnp.float32,
            )
            gram = term if t == 0 and r == 0 else gram + term
        pltpu.make_async_copy(w_ref.at[t], w_out.at[t], w_sem.at[t]).start()
    part[...] = gram.reshape(part.shape)

    copies = []
    for o in range(1, group):
        other = lax.rem(in_group + o, group)
        copy = pltpu.make_async_remote_copy(
            src_ref=part.at[other],
            dst_ref=piece.at[o - 1],
            send_sem=scatter_send.at[o - 1], recv_sem=scatter_recv.at[o - 1],
            device_id=(group_peer(o),), device_id_type=MESH,
        )
        copy.start()
        copies.append(copy)
    total = part[in_group]
    for o in range(1, group):
        copies[o - 1].wait_recv()
        total = total + piece[o - 1]
    sent += copies
    if groups > 1:
        gathered[group_id] = total
        copies = []
        for o in range(1, groups):
            copy = pltpu.make_async_remote_copy(
                src_ref=gathered.at[group_id], dst_ref=gathered.at[group_id],
                send_sem=cross_send.at[o - 1], recv_sem=cross_recv.at[o - 1],
                device_id=(cross_peer(o),), device_id_type=MESH,
            )
            copy.start()
            copies.append(copy)
        for copy in copies:
            copy.wait_recv()
        sent += copies
        total = gathered[0]
        for g in range(1, groups):
            total = total + gathered[g]
    gram_ref[in_group] = total * scale
    copies = []
    for o in range(1, group):
        copy = pltpu.make_async_remote_copy(
            src_ref=gram_ref.at[in_group], dst_ref=gram_ref.at[in_group],
            send_sem=gather_send.at[o - 1], recv_sem=gather_recv.at[o - 1],
            device_id=(group_peer(o),), device_id_type=MESH,
        )
        copy.start()
        copies.append(copy)
    for copy in copies:
        copy.wait_recv()
    for copy in sent + copies:
        copy.wait_send()
    for t in range(chunks):
        pltpu.make_async_copy(w_ref.at[t], w_out.at[t], w_sem.at[t]).wait()


def tiles_first(array):
    *lead, rows, cols = array.shape
    array = array.reshape(*lead, rows, cols // LANES, LANES)
    k = len(lead)
    order = tuple(range(k)) + (k + 1, k, k + 2)
    array = with_layout_constraint(array, Layout(major_to_minor=order))
    return jnp.swapaxes(array, -3, -2)


def vorticity_gram(velocity, n):
    _, snaps, rows, cols = velocity.shape
    chunks = cols // LANES
    group = GROUP if n % GROUP == 0 else 1
    groups = n // group
    height = snaps // group
    scale = 1.0 / (144.0 * n * rows * cols)
    flat = tiles_first(velocity).reshape(2, snaps * chunks * rows, LANES)
    dma = pltpu.SemaphoreType.DMA
    f32 = jnp.float32
    vmem = pl.BlockSpec(memory_space=pltpu.VMEM)
    return pl.pallas_call(
        functools.partial(gram_kernel, n, snaps, rows, chunks, group, scale),
        out_shape=(
            jax.ShapeDtypeStruct((chunks, rows, snaps, LANES), f32),
            jax.ShapeDtypeStruct((group, height, snaps), f32),
        ),
        in_specs=[pl.BlockSpec(memory_space=pl.ANY)],
        out_specs=(pl.BlockSpec(memory_space=pl.ANY), vmem),
        scratch_shapes=[
            pltpu.VMEM((chunks, rows, snaps, LANES), f32),
            pltpu.VMEM((2, snaps * chunks * rows, LANES), f32),
            pltpu.VMEM((chunks, rows, snaps, LANES), f32),
            pltpu.VMEM((chunks, 2, snaps, LANES), f32),
            pltpu.VMEM((chunks, 2, snaps, LANES), f32),
            pltpu.VMEM((group, height, snaps), f32),
            pltpu.VMEM((group - 1, height, snaps), f32),
            pltpu.VMEM((groups, height, snaps), f32),
            dma((2,)), dma((chunks,)),
            dma((chunks,)), dma((chunks,)), dma((chunks,)), dma((chunks,)),
            dma((group - 1,)), dma((group - 1,)),
            dma((max(groups - 1, 1),)), dma((max(groups - 1, 1),)),
            dma((group - 1,)), dma((group - 1,)),
        ],
        compiler_params=pltpu.CompilerParams(
            collective_id=0, has_side_effects=True, vmem_limit_bytes=58 * 1024 * 1024
        ),
        name="vorticity_gram",
    )(flat)


def modes_kernel(
    snaps, rows, chunks, parts, gram_ref, w_ref, out_ref, triangle_ref, inverse, out, out_sem
):
    blocks = snaps // 8
    size = snaps // parts
    span = size * rows * chunks
    copies = []
    sub = lax.broadcasted_iota(jnp.int32, (8, snaps), 0)
    lane = lax.broadcasted_iota(jnp.int32, (8, snaps), 1)
    left = [gram_ref[pl.ds(8 * b, 8), :] for b in range(blocks)]
    side = [jnp.where(lane == sub + 8 * b, 1.0, 0.0) for b in range(blocks)]

    for b in range(blocks):
        spread = [
            [jnp.broadcast_to(left[i][:, 8 * b + k : 8 * b + k + 1], (8, snaps)) for k in range(8)]
            for i in range(b, blocks)
        ]
        pivots = spread[0][0]
        for k in range(8):
            pivot = spread[0][k][k : k + 1, :]
            inv = 1.0 / pivot
            pivots = jnp.where(sub == k, spread[0][k], pivots)
            row_left = left[b][k : k + 1, :]
            row_side = side[b][k : k + 1, :]
            row_spread = [spread[0][q][k : k + 1, :] for q in range(k + 1, 8)]
            for i in range(b, blocks):
                mult = spread[i - b][k] * inv
                if i == b:
                    mult = jnp.where(sub > k, mult, 0.0)
                if i > b or k < 7:
                    left[i] = left[i] - mult * row_left
                    side[i] = side[i] - mult * row_side
                    for q in range(k + 1, 8):
                        spread[i - b][q] = spread[i - b][q] - mult * row_spread[q - k - 1]
        root = lax.rsqrt(pivots)
        here = pl.ds(8 * b, 8)
        triangle_ref[here, :] = jnp.where(lane >= sub + 8 * b, left[b] * root, 0.0)
        inverse[here, :] = side[b] * (root * (1.0 / 12.0))

        if (8 * b + 8) % size:
            continue
        p = b * 8 // size
        known = (p + 1) * size
        mine = inverse[pl.ds(p * size, size), :][:, :known]
        for t in range(chunks):
            for r in range(rows):
                out[pl.ds(p * span + t * rows + r, size, stride=rows * chunks), :] = jnp.dot(
                    mine, w_ref[t, r, pl.ds(0, known)],
                    precision=HIGHEST, preferred_element_type=jnp.float32,
                )
        copy = pltpu.make_async_copy(
            out.at[pl.ds(p * span, span)], out_ref.at[pl.ds(p * span, span)], out_sem.at[p]
        )
        copy.start()
        copies.append(copy)

    for copy in copies:
        copy.wait()


def modes_triangle(gram, w):
    chunks, rows, snaps, _ = w.shape
    parts = 2
    f32 = jnp.float32
    vmem = pl.BlockSpec(memory_space=pltpu.VMEM)
    return pl.pallas_call(
        functools.partial(modes_kernel, snaps, rows, chunks, parts),
        out_shape=(
            jax.ShapeDtypeStruct((snaps * chunks * rows, LANES), f32),
            jax.ShapeDtypeStruct((snaps, snaps), f32),
        ),
        in_specs=[vmem, vmem],
        out_specs=(pl.BlockSpec(memory_space=pl.ANY), vmem),
        scratch_shapes=[
            pltpu.VMEM((snaps, snaps), f32),
            pltpu.VMEM((snaps * chunks * rows, LANES), f32),
            pltpu.SemaphoreType.DMA((parts,)),
        ],
        compiler_params=pltpu.CompilerParams(vmem_limit_bytes=58 * 1024 * 1024),
        name="modes_triangle",
    )(gram, w)


def rows_first(array, snaps, rows, chunks):
    array = array.reshape(snaps, chunks, rows, LANES)
    array = jnp.swapaxes(array, 1, 2)
    array = with_layout_constraint(array, Layout(major_to_minor=(0, 2, 1, 3)))
    return array.reshape(snaps, rows, chunks * LANES)


def local(n, velocity):
    _, snaps, rows, cols = velocity.shape
    w, gram = vorticity_gram(velocity, n)
    gram = gram.reshape(snaps, snaps)
    modes, triangle = modes_triangle(gram, w)
    return rows_first(modes, snaps, rows, cols // LANES), triangle


def solution(mesh):
    return jax.shard_map(
        functools.partial(local, mesh.shape["strip"]),
        mesh=mesh,
        in_specs=(P(None, None, "strip", None),),
        out_specs=(P(None, "strip", None), P()),
        check_vma=False,
    )
```

```python
import functools

import jax
import jax.numpy as jnp
from jax import lax
from jax.experimental import pallas as pl
from jax.experimental.pallas import tpu as pltpu
from jax.experimental.layout import Layout, with_layout_constraint
from jax.sharding import PartitionSpec as P

LANES = 128
GROUP = 8
SLABS = 4
HIGHEST = lax.Precision.HIGHEST
MESH = pl.DeviceIdType.MESH


def gram_kernel(
    n, snaps, rows, chunks, group, scale,
    vel_ref, w_out, gram_ref,
    w_ref, vel, field, before, after, part, piece, gathered,
    load_sem, w_sem, up_send, up_recv, down_send, down_recv,
    scatter_send, scatter_recv, cross_send, cross_recv, gather_send, gather_recv,
):
    me = lax.axis_index("strip")
    right, left = lax.rem(me + 1, n), lax.rem(me + n - 1, n)
    in_group = lax.rem(me, group)
    base = me - in_group
    group_id = me // group
    groups = n // group
    stride = rows * chunks

    slab = snaps * stride // SLABS
    loads = [
        [
            pltpu.make_async_copy(
                vel_ref.at[c, pl.ds(i * slab, slab)],
                vel.at[c, pl.ds(i * slab, slab)],
                load_sem.at[c, i],
            )
            for i in range(SLABS)
        ]
        for c in (1, 0)
    ]
    for load in loads[0]:
        load.start()

    def group_peer(offset):
        return base + lax.rem(in_group + offset, group)

    def cross_peer(offset):
        return lax.rem(me + offset * group, n)

    barrier = pltpu.get_barrier_semaphore()
    greeted = [right, left]
    greeted += [group_peer(o) for o in range(1, group)]
    greeted += [cross_peer(o) for o in range(1, groups)]
    for peer in greeted:
        pl.semaphore_signal(barrier, inc=1, device_id=(peer,), device_id_type=MESH)
    for load in loads[0]:
        load.wait()
    for t in range(chunks):
        for r in range(rows):
            field[t, r] = vel[1, pl.ds(t * rows + r, snaps, stride=stride), :]
        if t == 0:
            pl.semaphore_wait(barrier, len(greeted))
        for src, dst, peer, send, recv in (
            (field.at[t, pl.ds(rows - 2, 2)], before.at[t], right, up_send, up_recv),
            (field.at[t, pl.ds(0, 2)], after.at[t], left, down_send, down_recv),
        ):
            pltpu.make_async_remote_copy(
                src_ref=src, dst_ref=dst, send_sem=send.at[t], recv_sem=recv.at[t],
                device_id=(peer,), device_id_type=MESH,
            ).start()
        if t == 0:
            for load in loads[1]:
                load.start()

    for load in loads[1]:
        load.wait()
    step = 16
    cols = chunks * LANES

    @pl.loop(0, snaps // step)
    def _(block):
        first = block * step
        for r in range(rows):
            row = jnp.concatenate(
                [
                    vel[0, pl.ds(first * stride + t * rows + r, step, stride=stride), :]
                    for t in range(chunks)
                ],
                axis=1,
            )
            wide = row - pltpu.roll(row, 2, 1)
            nine = 8.0 * wide - pltpu.roll(wide, cols - 1, 1)
            along = pltpu.roll(nine, cols - 1, 1) - wide
            for t in range(chunks):
                here = pl.ds(first, step)
                out = -along[:, t * LANES : (t + 1) * LANES]
                for shift, weight in ((1, 8.0), (-1, -8.0), (2, -1.0), (-2, 1.0)):
                    if 0 <= r + shift < rows:
                        out = out + weight * field[t, r + shift, here]
                w_ref[t, r, here] = out

    sent = []
    for t in range(chunks):
        up = pltpu.make_async_remote_copy(
            src_ref=field.at[t, pl.ds(rows - 2, 2)], dst_ref=before.at[t],
            send_sem=up_send.at[t], recv_sem=up_recv.at[t],
            device_id=(right,), device_id_type=MESH,
        )
        down = pltpu.make_async_remote_copy(
            src_ref=field.at[t, pl.ds(0, 2)], dst_ref=after.at[t],
            send_sem=down_send.at[t], recv_sem=down_recv.at[t],
            device_id=(left,), device_id_type=MESH,
        )
        up.wait_recv()
        down.wait_recv()
        sent += [up, down]
        for r in range(rows):
            out = w_ref[t, r]
            for shift, weight in ((1, 8.0), (-1, -8.0), (2, -1.0), (-2, 1.0)):
                if r + shift < 0:
                    out = out + weight * before[t, r + shift + 2]
                elif r + shift >= rows:
                    out = out + weight * after[t, r + shift - rows]
            w_ref[t, r] = out
            term = lax.dot_general(
                out, out, (((1,), (1,)), ((), ())),
                precision=HIGHEST, preferred_element_type=jnp.float32,
            )
            gram = term if t == 0 and r == 0 else gram + term
        pltpu.make_async_copy(w_ref.at[t], w_out.at[t], w_sem.at[t]).start()
    part[...] = gram.reshape(part.shape)

    copies = []
    for o in range(1, group):
        other = lax.rem(in_group + o, group)
        copy = pltpu.make_async_remote_copy(
            src_ref=part.at[other],
            dst_ref=piece.at[o - 1],
            send_sem=scatter_send.at[o - 1], recv_sem=scatter_recv.at[o - 1],
            device_id=(group_peer(o),), device_id_type=MESH,
        )
        copy.start()
        copies.append(copy)
    total = part[in_group]
    for o in range(1, group):
        copies[o - 1].wait_recv()
        total = total + piece[o - 1]
    sent += copies
    if groups > 1:
        gathered[group_id] = total
        copies = []
        for o in range(1, groups):
            copy = pltpu.make_async_remote_copy(
                src_ref=gathered.at[group_id], dst_ref=gathered.at[group_id],
                send_sem=cross_send.at[o - 1], recv_sem=cross_recv.at[o - 1],
                device_id=(cross_peer(o),), device_id_type=MESH,
            )
            copy.start()
            copies.append(copy)
        for copy in copies:
            copy.wait_recv()
        sent += copies
        total = gathered[0]
        for g in range(1, groups):
            total = total + gathered[g]
    gram_ref[in_group] = total * scale
    copies = []
    for o in range(1, group):
        copy = pltpu.make_async_remote_copy(
            src_ref=gram_ref.at[in_group], dst_ref=gram_ref.at[in_group],
            send_sem=gather_send.at[o - 1], recv_sem=gather_recv.at[o - 1],
            device_id=(group_peer(o),), device_id_type=MESH,
        )
        copy.start()
        copies.append(copy)
    for copy in copies:
        copy.wait_recv()
    for copy in sent + copies:
        copy.wait_send()
    for t in range(chunks):
        pltpu.make_async_copy(w_ref.at[t], w_out.at[t], w_sem.at[t]).wait()


def tiles_first(array):
    *lead, rows, cols = array.shape
    array = array.reshape(*lead, rows, cols // LANES, LANES)
    k = len(lead)
    order = tuple(range(k)) + (k + 1, k, k + 2)
    array = with_layout_constraint(array, Layout(major_to_minor=order))
    return jnp.swapaxes(array, -3, -2)


def vorticity_gram(velocity, n):
    _, snaps, rows, cols = velocity.shape
    chunks = cols // LANES
    group = GROUP if n % GROUP == 0 else 1
    groups = n // group
    height = snaps // group
    scale = 1.0 / (144.0 * n * rows * cols)
    flat = tiles_first(velocity).reshape(2, snaps * chunks * rows, LANES)
    dma = pltpu.SemaphoreType.DMA
    f32 = jnp.float32
    vmem = pl.BlockSpec(memory_space=pltpu.VMEM)
    return pl.pallas_call(
        functools.partial(gram_kernel, n, snaps, rows, chunks, group, scale),
        out_shape=(
            jax.ShapeDtypeStruct((chunks, rows, snaps, LANES), f32),
            jax.ShapeDtypeStruct((group, height, snaps), f32),
        ),
        in_specs=[pl.BlockSpec(memory_space=pl.ANY)],
        out_specs=(pl.BlockSpec(memory_space=pl.ANY), vmem),
        scratch_shapes=[
            pltpu.VMEM((chunks, rows, snaps, LANES), f32),
            pltpu.VMEM((2, snaps * chunks * rows, LANES), f32),
            pltpu.VMEM((chunks, rows, snaps, LANES), f32),
            pltpu.VMEM((chunks, 2, snaps, LANES), f32),
            pltpu.VMEM((chunks, 2, snaps, LANES), f32),
            pltpu.VMEM((group, height, snaps), f32),
            pltpu.VMEM((group - 1, height, snaps), f32),
            pltpu.VMEM((groups, height, snaps), f32),
            dma((2, SLABS)), dma((chunks,)),
            dma((chunks,)), dma((chunks,)), dma((chunks,)), dma((chunks,)),
            dma((group - 1,)), dma((group - 1,)),
            dma((max(groups - 1, 1),)), dma((max(groups - 1, 1),)),
            dma((group - 1,)), dma((group - 1,)),
        ],
        compiler_params=pltpu.CompilerParams(
            collective_id=0, has_side_effects=True, vmem_limit_bytes=58 * 1024 * 1024
        ),
        name="vorticity_gram",
    )(flat)


def modes_kernel(
    snaps, rows, chunks, parts, gram_ref, w_ref, out_ref, triangle_ref, inverse, out, out_sem
):
    blocks = snaps // 8
    size = snaps // parts
    span = size * rows * chunks
    copies = []
    sub = lax.broadcasted_iota(jnp.int32, (8, snaps), 0)
    lane = lax.broadcasted_iota(jnp.int32, (8, snaps), 1)
    left = [gram_ref[pl.ds(8 * b, 8), :] for b in range(blocks)]
    side = [jnp.where(lane == sub + 8 * b, 1.0, 0.0) for b in range(blocks)]

    for b in range(blocks):
        spread = [
            [jnp.broadcast_to(left[i][:, 8 * b + k : 8 * b + k + 1], (8, snaps)) for k in range(8)]
            for i in range(b, blocks)
        ]
        pivots = spread[0][0]
        for k in range(8):
            pivot = spread[0][k][k : k + 1, :]
            inv = 1.0 / pivot
            pivots = jnp.where(sub == k, spread[0][k], pivots)
            row_left = left[b][k : k + 1, :]
            row_side = side[b][k : k + 1, :]
            row_spread = [spread[0][q][k : k + 1, :] for q in range(k + 1, 8)]
            for i in range(b, blocks):
                mult = spread[i - b][k] * inv
                if i == b:
                    mult = jnp.where(sub > k, mult, 0.0)
                if i > b or k < 7:
                    left[i] = left[i] - mult * row_left
                    side[i] = side[i] - mult * row_side
                    for q in range(k + 1, 8):
                        spread[i - b][q] = spread[i - b][q] - mult * row_spread[q - k - 1]
        root = lax.rsqrt(pivots)
        here = pl.ds(8 * b, 8)
        triangle_ref[here, :] = jnp.where(lane >= sub + 8 * b, left[b] * root, 0.0)
        inverse[here, :] = side[b] * (root * (1.0 / 12.0))

        if (8 * b + 8) % size:
            continue
        p = b * 8 // size
        known = (p + 1) * size
        mine = inverse[pl.ds(p * size, size), :][:, :known]
        for t in range(chunks):
            for r in range(rows):
                out[pl.ds(p * span + t * rows + r, size, stride=rows * chunks), :] = jnp.dot(
                    mine, w_ref[t, r, pl.ds(0, known)],
                    precision=HIGHEST, preferred_element_type=jnp.float32,
                )
        copy = pltpu.make_async_copy(
            out.at[pl.ds(p * span, span)], out_ref.at[pl.ds(p * span, span)], out_sem.at[p]
        )
        copy.start()
        copies.append(copy)

    for copy in copies:
        copy.wait()


def modes_triangle(gram, w):
    chunks, rows, snaps, _ = w.shape
    parts = 2
    f32 = jnp.float32
    vmem = pl.BlockSpec(memory_space=pltpu.VMEM)
    return pl.pallas_call(
        functools.partial(modes_kernel, snaps, rows, chunks, parts),
        out_shape=(
            jax.ShapeDtypeStruct((snaps * chunks * rows, LANES), f32),
            jax.ShapeDtypeStruct((snaps, snaps), f32),
        ),
        in_specs=[vmem, vmem],
        out_specs=(pl.BlockSpec(memory_space=pl.ANY), vmem),
        scratch_shapes=[
            pltpu.VMEM((snaps, snaps), f32),
            pltpu.VMEM((snaps * chunks * rows, LANES), f32),
            pltpu.SemaphoreType.DMA((parts,)),
        ],
        compiler_params=pltpu.CompilerParams(vmem_limit_bytes=58 * 1024 * 1024),
        name="modes_triangle",
    )(gram, w)


def rows_first(array, snaps, rows, chunks):
    array = array.reshape(snaps, chunks, rows, LANES)
    array = jnp.swapaxes(array, 1, 2)
    array = with_layout_constraint(array, Layout(major_to_minor=(0, 2, 1, 3)))
    return array.reshape(snaps, rows, chunks * LANES)


def local(n, velocity):
    _, snaps, rows, cols = velocity.shape
    w, gram = vorticity_gram(velocity, n)
    gram = gram.reshape(snaps, snaps)
    modes, triangle = modes_triangle(gram, w)
    return rows_first(modes, snaps, rows, cols // LANES), triangle


def solution(mesh):
    return jax.shard_map(
        functools.partial(local, mesh.shape["strip"]),
        mesh=mesh,
        in_specs=(P(None, None, "strip", None),),
        out_specs=(P(None, "strip", None), P()),
        check_vma=False,
    )
```
